32 devices in a mesh: region: 4 (over y, core), cols: 8 (over z, x).
Axes of the slice: x: 2, y: 2, z: 4, core: 2. Of those that a mesh axis runs over, the one named last changes fastest.
Arguments:
- incidence: bfloat16 [4, 8, 8, 128, 1024], P('region', 'cols'), may hold values from 0 to 1, as said below
- tile_rows: int32 [4, 8, 8], P('region', 'cols'), may hold values from 0 to 63, as said below
- tile_cols: int32 [4, 8, 8], P('region', 'cols'), may hold values from 0 to 63, as said below
- tile_count: int32 [4, 8], P('region', 'cols'), may hold values from 1 to 8, as said below
- route_cost: float32 [524288], P('cols'), may hold values from 1 to 18
- primal: float32 [524288], P('cols'), may hold values from 0 to 1
- duals: float32 [32768], P('region'), may hold values from -6 to 6
- balance: float32 [], replicated, may hold values from 0.2 to 0.8
Outputs:
- primal_next: float32 [524288], P('cols')
- duals_next: float32 [32768], P('region')
- balance_next: float32 [], replicated
The draws below stay inside these ranges and needn't reach their ends.
Inputs may be any that keep to these rules, and one draw needn't show every extreme that they name: `incidence`: entries are 0 or 1. On one device the (tile_rows, tile_cols) pairs of its slots are distinct. On one device the (tile_rows, tile_cols) pairs of its slots are distinct. Slots from tile_count on hold no part of A; on every region index some device has all 8 slots live.
All inputs are finite; a program needn't handle non-finite values.
Results may differ from the reference program's by a relative error of at most 0.0003.
Values sent between devices are 32-bit elements; how exact they have to be, the bound alone decides.
A program may use at most 64 MiB of HBM per device.

```python
import math
import jax
import jax.numpy as jnp
from jax import lax

TILE_R = 128
TILE_C = 1024
RB_DEV = 64
CB_DEV = 64
SLOTS = 8
ITERS = 2
REGIONS = 4
COLGROUPS = 8
ROWS = 32768
COLUMNS = 524288


def permute_pairs(single_key):
    return jax.random.permutation(single_key, RB_DEV * CB_DEV)


def pair_picks(key):
    devices = REGIONS * COLGROUPS
    pairs = RB_DEV * CB_DEV
    keys = jax.random.split(key, devices + 1)
    perms = jax.vmap(permute_pairs)(keys[:devices]).astype(jnp.int32)
    first = jax.random.randint(keys[devices], (), 0, devices)
    second = (first + 1) % devices
    device_ids = jnp.arange(devices, dtype=jnp.int32)
    target = jnp.where(device_ids == first, pairs - 1, jnp.where(device_ids == second, 0, -1))
    located = jnp.argmax(perms == target[:, None], axis=1).astype(jnp.int32)
    shifted = (jnp.arange(pairs, dtype=jnp.int32)[None, :] + located[:, None]) % pairs
    rolled = jnp.take_along_axis(perms, shifted, axis=1)
    return rolled[:, :SLOTS].reshape(REGIONS, COLGROUPS, SLOTS).astype(jnp.int32)


def draw_tile_rows(key, part):
    picks = pair_picks(key)
    return (picks // CB_DEV).astype(jnp.int32)


def draw_tile_cols(key, part):
    picks = pair_picks(key)
    return (picks % CB_DEV).astype(jnp.int32)


def draw_tile_count(key, part):
    key = jax.random.fold_in(key, 3)
    key_base, key_full = jax.random.split(key)
    base = jax.random.randint(key_base, (REGIONS, COLGROUPS), 1, max(SLOTS // 2, 1) + 1)
    fullest = jax.random.randint(key_full, (REGIONS,), 0, COLGROUPS)
    column = jnp.arange(COLGROUPS, dtype=jnp.int32)[None, :]
    lightest = (fullest + 1) % COLGROUPS
    counts = jnp.where(column == fullest[:, None], SLOTS, jnp.where(column == lightest[:, None], 1, base))
    return counts.astype(jnp.int32)


def draw_incidence(key, part):
    key = jax.random.fold_in(key, 5)
    hits = jax.random.randint(key, (REGIONS, COLGROUPS, SLOTS, TILE_R, TILE_C), 0, 8) == 0
    return hits.astype(jnp.bfloat16)


def draw_route_cost(key, part):
    key = jax.random.fold_in(key, 7)
    position = jnp.arange(COLUMNS, dtype=jnp.float32) / (COLUMNS - 1)
    ramp = 1.0 + 2.0 * position
    factor = jax.random.uniform(key, (COLUMNS,), jnp.float32, 1.0, 6.0)
    return (ramp * factor).astype(jnp.float32)


def steps_of(key, extent, pieces, least, largest):
    def one(dim, blocks):
        heights = jax.random.uniform(jax.random.fold_in(jax.random.fold_in(key, 6), dim), (blocks,), jnp.float32, least / len(pieces), largest / len(pieces))
        return jnp.repeat(jnp.exp(heights), extent[dim] // blocks).reshape((-1,) + (1,) * (len(extent) - dim - 1))

    factor_of = one(*pieces[0])
    for cut in pieces[1:]:
        factor_of = factor_of * one(*cut)
    return factor_of


def noise(key, dims, deviation, bound, shards=(), held_as=jnp.bfloat16):
    result = jax.random.normal(key, dims, jnp.float32) * deviation
    if len(shards) > 0:
        result = steps_of(key, dims, shards, -0.22, 0.18) * result
    return jnp.clip(result, min=-bound, max=bound).astype(held_as)


def setup_inputs(seed: int = 0) -> dict:
    arg_keys = jax.random.split(jax.random.key(seed), 9)
    incidence = draw_incidence(jax.random.fold_in(arg_keys[8], 71), 0)
    tile_rows = draw_tile_rows(jax.random.fold_in(arg_keys[8], 71), 0)
    tile_cols = draw_tile_cols(jax.random.fold_in(arg_keys[8], 71), 0)
    tile_count = draw_tile_count(jax.random.fold_in(arg_keys[8], 71), 0)
    route_cost = draw_route_cost(jax.random.fold_in(arg_keys[8], 71), 0)
    primal = jnp.clip(1.0 * jax.random.uniform(arg_keys[5], (COLUMNS,), jnp.float32) ** steps_of(arg_keys[5], (COLUMNS,), ((0, 8),), -0.2, 0.2), 0.0, 1.0)
    duals = noise(arg_keys[6], (ROWS,), 1.0, 6.0, ((0, 4),), jnp.float32)
    balance = jnp.clip(jnp.exp(jax.random.uniform(arg_keys[7], (), jnp.float32, math.log(0.2), math.log(0.8))), 0.2, 0.8)
    return {"incidence": incidence, "tile_rows": tile_rows, "tile_cols": tile_cols, "tile_count": tile_count, "route_cost": route_cost, "primal": primal, "duals": duals, "balance": balance}


step_scale = 0.012
epsilon = 1e-06
highest = lax.Precision.HIGHEST

def slot_live(tile_count):
    return jnp.arange(SLOTS, dtype=jnp.int32)[None, None, :] < tile_count[:, :, None]

def transpose_product(incidence, tile_rows, tile_cols, live_slots, duals):
    dual_blocks = duals.reshape(REGIONS, RB_DEV, TILE_R)

    def region_step(running, inputs):
        region_tiles, region_rows, region_cols, region_live, region_duals = inputs
        dual_rows = region_duals[region_rows]
        products = jnp.einsum('csij,csi->csj', region_tiles.astype(jnp.float32), dual_rows, precision=highest)
        col_pick = ((region_cols[..., None] == jnp.arange(CB_DEV, dtype=jnp.int32)) & region_live[..., None]).astype(jnp.float32)
        return (running + jnp.einsum('csb,csj->cbj', col_pick, products, precision=highest), None)
    initial = jnp.zeros((COLGROUPS, CB_DEV, TILE_C), jnp.float32)
    summed, ignored = lax.scan(region_step, initial, (incidence, tile_rows, tile_cols, live_slots, dual_blocks))
    return summed.reshape(-1)

def forward_product(incidence, tile_rows, tile_cols, live_slots, field):
    field_blocks = field.reshape(COLGROUPS, CB_DEV, TILE_C)
    groups = jnp.arange(COLGROUPS, dtype=jnp.int32)[:, None]

    def region_step(inputs):
        region_tiles, region_rows, region_cols, region_live = inputs
        primal_cols = field_blocks[groups, region_cols]
        products = jnp.einsum('csij,csj->csi', region_tiles.astype(jnp.float32), primal_cols, precision=highest)
        row_pick = ((region_rows[..., None] == jnp.arange(RB_DEV, dtype=jnp.int32)) & region_live[..., None]).astype(jnp.float32)
        return jnp.einsum('csr,csi->ri', row_pick, products, precision=highest)
    return lax.map(region_step, (incidence, tile_rows, tile_cols, live_slots)).reshape(-1)

def reference(incidence, tile_rows, tile_cols, tile_count, route_cost, primal, duals, balance):
    live_slots = slot_live(tile_count)
    for iteration in range(ITERS):
        primal_step = step_scale / balance
        dual_step = step_scale * balance
        reduced = route_cost - transpose_product(incidence, tile_rows, tile_cols, live_slots, duals)
        moved = jnp.clip(primal - primal_step * reduced, 0.0, 1.0)
        extrapolated = 2.0 * moved - primal
        coverage = forward_product(incidence, tile_rows, tile_cols, live_slots, extrapolated)
        updated = duals + dual_step * (1.0 - coverage)
        primal_moves = jnp.sum((moved - primal) ** 2)
        dual_moves = jnp.sum((updated - duals) ** 2)
        balance = jnp.sqrt(balance * jnp.sqrt((dual_moves + epsilon) / (primal_moves + epsilon)))
        primal = moved
        duals = updated
    return (primal, duals, balance)
```

```python
import functools

import jax
import jax.numpy as jnp
from jax import lax
from jax.experimental import pallas as pl
from jax.experimental.pallas import tpu as pltpu
from jax.sharding import PartitionSpec as P

ITERS = 2

step_scale = 0.012
epsilon = 1e-06
MESH = pl.DeviceIdType.MESH
LANES = 128
SUB = 8


def split(value):
    high = value.astype(jnp.bfloat16).astype(jnp.float32)
    rest = value - high
    middle = rest.astype(jnp.bfloat16).astype(jnp.float32)
    return high, middle, rest - middle


def stacked(value):
    high, middle, low = split(value)
    rows = jnp.concatenate([high, middle, low, jnp.zeros_like(value)], axis=0)
    return rows.astype(jnp.bfloat16)


def unstacked(product):
    return product[2 * SUB : 3 * SUB] + product[SUB : 2 * SUB] + product[:SUB]


def scatter(picks, blocks):
    sides = [term.astype(jnp.bfloat16) for term in split(blocks)]
    product = jnp.dot(
        picks, jnp.concatenate(sides, axis=1), preferred_element_type=jnp.float32
    )
    return product[:, 2 * LANES :] + product[:, LANES : 2 * LANES] + product[:, :LANES]


def folded(value):
    return jnp.sum(value.reshape(-1, SUB, LANES), axis=0)


def kernel(
    regions, groups,
    tile_rows, tile_cols, tile_count, balance,
    incidence_hbm, cost_hbm, primal_hbm, duals_hbm,
    primal_out, duals_out, balance_out,
    tiles, cost, x, y, extrapolated, dual_rows, primal_cols,
    col_picks, row_picks, col_box, row_box, last_box,
    load_sem, store_sem,
    col_send, col_recv, row_send, row_recv, last_send, last_recv,
):
    region, group = lax.axis_index("region"), lax.axis_index("cols")
    width = tiles.shape[1]
    chunks = width // LANES

    loads = [
        pltpu.make_async_copy(source, target, load_sem.at[i])
        for i, (source, target) in enumerate(
            ((duals_hbm, y), (incidence_hbm, tiles), (primal_hbm, x), (cost_hbm, cost))
        )
    ]
    for load in loads:
        load.start()

    region_peers = [lax.rem(region + d, regions) for d in range(1, regions)]
    group_peers = [lax.rem(group + d, groups) for d in range(1, groups)]
    barrier = pltpu.get_barrier_semaphore()
    for peer in region_peers:
        pl.semaphore_signal(barrier, inc=1, device_id=(peer, group), device_id_type=MESH)
    for peer in group_peers:
        pl.semaphore_signal(barrier, inc=1, device_id=(region, peer), device_id_type=MESH)

    def region_copy(box, send, recv, owner, peer, send_slot):
        return pltpu.make_async_remote_copy(
            src_ref=box.at[owner], dst_ref=box.at[owner],
            send_sem=send.at[send_slot], recv_sem=recv.at[owner],
            device_id=(peer, group), device_id_type=MESH,
        )

    def group_copy(box, send, recv, owner, peer, send_slot):
        return pltpu.make_async_remote_copy(
            src_ref=box.at[owner], dst_ref=box.at[owner],
            send_sem=send.at[send_slot], recv_sem=recv.at[owner],
            device_id=(region, peer), device_id_type=MESH,
        )

    pending = []

    def exchange(copy, me, peers, box, send, recv):
        for slot, peer in enumerate(peers):
            sent = copy(box, send, recv, me, peer, slot)
            sent.start()
            pending.append(sent)

    def arrive(copy, peers, box, send, recv):
        for slot, peer in enumerate(peers):
            copy(box, send, recv, peer, peer, slot).wait_recv()

    lane = lax.broadcasted_iota(jnp.int32, (SUB, LANES), 1)
    sub = lax.broadcasted_iota(jnp.int32, (SUB, LANES), 0)
    rows_of, cols_of = [], []
    col_marks = jnp.full((SUB, LANES), -1, jnp.int32)
    row_marks = jnp.full((SUB, LANES), -1, jnp.int32)
    for s in range(SUB):
        rows_of.append(tile_rows[0, 0, s])
        cols_of.append(tile_cols[0, 0, s])
        mine = jnp.logical_and(lane % SUB == s, s < jnp.full((SUB, LANES), tile_count[0, 0]))
        col_marks = jnp.where(mine, cols_of[s] * chunks + (lane // SUB) % chunks, col_marks)
        row_marks = jnp.where(mine, rows_of[s], row_marks)

    weight = jnp.full((1, 1), balance[0], jnp.float32)
    half = SUB * chunks
    pl.semaphore_wait(barrier, regions + groups - 2)

    for iteration in range(ITERS):
        cbox, csend, crecv = col_box.at[iteration], col_send.at[iteration], col_recv.at[iteration]
        rbox, rsend, rrecv = row_box.at[iteration], row_send.at[iteration], row_recv.at[iteration]
        dual_step = step_scale * weight

        if iteration == 0:
            loads[0].wait()
        for s in range(SUB):
            dual_rows[s] = y[rows_of[s]]
        picked = dual_rows[...]
        diagonal = jnp.concatenate([jnp.where(sub == s, picked, 0.0) for s in range(SUB)], axis=1)
        if iteration == 0:
            loads[1].wait()
        products = unstacked(
            jnp.dot(stacked(diagonal), tiles[...], preferred_element_type=jnp.float32)
        )
        for k in range(chunks):
            cbox[region, k * SUB : (k + 1) * SUB, :] = products[:, k * LANES : (k + 1) * LANES]
        if iteration == 0:
            cbox[region, half : half + SUB, :] = col_marks.astype(jnp.float32)
        else:
            cbox[region, half : half + SUB, :] = dual_moves
        exchange(region_copy, region, region_peers, cbox, csend, crecv)
        if iteration == 0:
            loads[2].wait()
            loads[3].wait()
        arrive(region_copy, region_peers, cbox, csend, crecv)

        if iteration == 0:
            place = lax.broadcasted_iota(jnp.int32, (x.shape[0], LANES), 0).astype(jnp.float32)
            spot = lax.broadcasted_iota(jnp.int32, (1, LANES), 1)
            per = LANES // half
            for j in range(regions // per):
                marks = cbox[j * per, half : half + 1, :]
                for i in range(1, per):
                    marks = jnp.where(spot // half == i, cbox[j * per + i, half : half + 1, :], marks)
                col_picks[:, j * LANES : (j + 1) * LANES] = jnp.where(
                    place == marks, 1.0, 0.0
                ).astype(jnp.bfloat16)
        else:
            dual_total = cbox[0, half : half + SUB, :]
            for r in range(1, regions):
                dual_total = dual_total + cbox[r, half : half + SUB, :]
            dual_total = jnp.sum(dual_total, axis=(0, 1), keepdims=True)
            weight = jnp.sqrt(
                weight * jnp.sqrt((dual_total + epsilon) / (primal_total + epsilon))
            )
            dual_step = step_scale * weight
        primal_step = step_scale / weight
        blocks = jnp.concatenate([cbox[r, :half, :] for r in range(regions)], axis=0)
        col_total = scatter(col_picks[...], blocks)
        before = x[...]
        moved = jnp.clip(before - primal_step * (cost[...] - col_total), 0.0, 1.0)
        x[...] = moved
        extrapolated[...] = (2.0 * moved - before).reshape(extrapolated.shape)
        if iteration == ITERS - 1:
            keep = pltpu.make_async_copy(x, primal_out, store_sem)
            keep.start()

        for s in range(SUB):
            primal_cols[s * chunks : (s + 1) * chunks, :] = extrapolated[cols_of[s]]
        routes = jnp.concatenate(
            [primal_cols[pl.ds(k, SUB, stride=chunks), :] for k in range(chunks)], axis=1
        )
        products = unstacked(
            lax.dot_general(
                stacked(routes), tiles[...], (((1,), (1,)), ((), ())),
                preferred_element_type=jnp.float32,
            )
        )
        own = jnp.where(sub == 0, products[:, :LANES], 0.0)
        for s in range(1, SUB):
            own = jnp.where(sub == s, products[:, s * LANES : (s + 1) * LANES], own)
        rbox[group, :SUB, :] = own
        rbox[group, SUB : 2 * SUB, :] = folded((moved - before) ** 2)
        rbox[group, 2 * SUB : 3 * SUB, :] = row_marks.astype(jnp.float32)
        exchange(group_copy, group, group_peers, rbox, rsend, rrecv)
        arrive(group_copy, group_peers, rbox, rsend, rrecv)

        if iteration == 0:
            span = row_picks.shape[1]
            piece = min(span, LANES)
            place = lax.broadcasted_iota(jnp.int32, (y.shape[0], piece), 0).astype(jnp.float32)
            spot = lax.broadcasted_iota(jnp.int32, (1, piece), 1)
            per = piece // SUB
            for j in range(span // piece):
                marks = rbox[j * per, 2 * SUB : 2 * SUB + 1, :piece]
                for i in range(1, per):
                    marks = jnp.where(
                        spot // SUB == i, rbox[j * per + i, 2 * SUB : 2 * SUB + 1, :piece], marks
                    )
                row_picks[:, j * piece : (j + 1) * piece] = jnp.where(
                    place == marks, 1.0, 0.0
                ).astype(jnp.bfloat16)
        blocks = jnp.concatenate([rbox[c, :SUB, :] for c in range(groups)], axis=0)
        coverage = scatter(row_picks[...], blocks)
        held = y[...]
        updated = held + dual_step * (1.0 - coverage)
        y[...] = updated
        dual_moves = folded((updated - held) ** 2)
        if iteration == ITERS - 1:
            last_box[region, :, :] = dual_moves
            exchange(region_copy, region, region_peers, last_box, last_send, last_recv)
            duals_out[...] = updated
        primal_total = rbox[0, SUB : 2 * SUB, :]
        for c in range(1, groups):
            primal_total = primal_total + rbox[c, SUB : 2 * SUB, :]
        primal_total = jnp.sum(primal_total, axis=(0, 1), keepdims=True)

    arrive(region_copy, region_peers, last_box, last_send, last_recv)
    dual_total = last_box[0]
    for r in range(1, regions):
        dual_total = dual_total + last_box[r]
    dual_total = jnp.sum(dual_total, axis=(0, 1), keepdims=True)
    balance_out[...] = jnp.sqrt(
        weight * jnp.sqrt((dual_total + epsilon) / (primal_total + epsilon))
    )
    for sent in pending:
        sent.wait_send()
    keep.wait()


def local(regions, groups, incidence, tile_rows, tile_cols, tile_count, route_cost, primal, duals, balance):
    slots, height, width = incidence.shape[2:]
    assert slots == SUB and height == LANES and width % LANES == 0
    chunks = width // LANES
    wide = (primal.shape[0] // LANES, LANES)
    tall = (duals.shape[0] // LANES, LANES)
    f32 = jnp.float32
    dma = pltpu.SemaphoreType.DMA
    smem = pl.BlockSpec(memory_space=pltpu.SMEM)
    vmem = pl.BlockSpec(memory_space=pltpu.VMEM)
    hbm = pl.BlockSpec(memory_space=pl.ANY)
    outs = pl.pallas_call(
        functools.partial(kernel, regions, groups),
        out_shape=(
            jax.ShapeDtypeStruct(wide, f32),
            jax.ShapeDtypeStruct(tall, f32),
            jax.ShapeDtypeStruct((1, 1), f32),
        ),
        in_specs=[smem] * 4 + [hbm] * 4,
        out_specs=(hbm, vmem, vmem),
        scratch_shapes=[
            pltpu.VMEM((slots * height, width), jnp.bfloat16),
            pltpu.VMEM(wide, f32),
            pltpu.VMEM(wide, f32),
            pltpu.VMEM(tall, f32),
            pltpu.VMEM((wide[0] // chunks, chunks, LANES), f32),
            pltpu.VMEM((SUB, LANES), f32),
            pltpu.VMEM((slots * chunks, LANES), f32),
            pltpu.VMEM((wide[0], regions * slots * chunks), jnp.bfloat16),
            pltpu.VMEM((tall[0], groups * slots), jnp.bfloat16),
            pltpu.VMEM((ITERS, regions, slots * chunks + SUB, LANES), f32),
            pltpu.VMEM((ITERS, groups, 3 * SUB, LANES), f32),
            pltpu.VMEM((regions, SUB, LANES), f32),
            dma((4,)),
            dma,
            dma((ITERS, regions)),
            dma((ITERS, regions)),
            dma((ITERS, groups)),
            dma((ITERS, groups)),
            dma((regions,)),
            dma((regions,)),
        ],
        compiler_params=pltpu.CompilerParams(
            collective_id=0, has_side_effects=True, vmem_limit_bytes=40 * 1024 * 1024
        ),
    )(
        tile_rows, tile_cols, tile_count, balance.reshape(1),
        incidence.reshape(slots * height, width),
        route_cost.reshape(wide), primal.reshape(wide), duals.reshape(tall),
    )
    return outs[0].reshape(-1), outs[1].reshape(-1), outs[2].reshape(())


def solution(mesh):
    return jax.shard_map(
        functools.partial(local, mesh.shape["region"], mesh.shape["cols"]),
        mesh=mesh,
        in_specs=(
            P("region", "cols", None, None, None),
            P("region", "cols", None),
            P("region", "cols", None),
            P("region", "cols"),
            P("cols"),
            P("cols"),
            P("region"),
            P(),
        ),
        out_specs=(P("cols"), P("region"), P()),
        check_vma=False,
    )
```

```python
import functools

import jax
import jax.numpy as jnp
from jax import lax
from jax.experimental import pallas as pl
from jax.experimental.pallas import tpu as pltpu
from jax.sharding import PartitionSpec as P

ITERS = 2

step_scale = 0.012
epsilon = 1e-06
MESH = pl.DeviceIdType.MESH
LANES = 128
SUB = 8


def split(value):
    high = value.astype(jnp.bfloat16).astype(jnp.float32)
    rest = value - high
    middle = rest.astype(jnp.bfloat16).astype(jnp.float32)
    return high, middle, rest - middle


def stacked(value):
    high, middle, low = split(value)
    rows = jnp.concatenate([high, middle, low, jnp.zeros_like(value)], axis=0)
    return rows.astype(jnp.bfloat16)


def unstacked(product):
    return product[2 * SUB : 3 * SUB] + product[SUB : 2 * SUB] + product[:SUB]


def scatter(picks, blocks):
    sides = [term.astype(jnp.bfloat16) for term in split(blocks)]
    product = jnp.dot(
        picks, jnp.concatenate(sides, axis=1), preferred_element_type=jnp.float32
    )
    return product[:, 2 * LANES :] + product[:, LANES : 2 * LANES] + product[:, :LANES]


def folded(value):
    return jnp.sum(jnp.sum(value.reshape(-1, SUB, LANES), axis=0), axis=0, keepdims=True)


def kernel(
    regions, groups,
    tile_rows_hbm, tile_cols_hbm, tile_count_hbm, balance_hbm,
    incidence_hbm, cost_hbm, primal_hbm, duals_hbm,
    primal_out, duals_out, balance_out,
    tile_rows, tile_cols, tile_count, balance,
    tiles, cost, x, y, extrapolated, dual_rows, primal_cols,
    col_picks, row_picks, col_box, row_box, last_box, final_weight,
    load_sem, store_sem,
    col_send, col_recv, row_send, row_recv, last_send, last_recv,
):
    region, group = lax.axis_index("region"), lax.axis_index("cols")
    width = tiles.shape[1]
    chunks = width // LANES

    loads = [
        pltpu.make_async_copy(source, target, load_sem.at[i])
        for i, (source, target) in enumerate(
            (
                (duals_hbm, y), (incidence_hbm, tiles), (primal_hbm, x), (cost_hbm, cost),
                (tile_rows_hbm, tile_rows), (tile_cols_hbm, tile_cols),
                (tile_count_hbm, tile_count), (balance_hbm, balance),
            )
        )
    ]
    for load in loads[4:] + loads[:4]:
        load.start()

    region_peers = [lax.rem(region + d, regions) for d in range(1, regions)]
    group_peers = [lax.rem(group + d, groups) for d in range(1, groups)]
    barrier = pltpu.get_barrier_semaphore()
    for peer in region_peers:
        pl.semaphore_signal(barrier, inc=1, device_id=(peer, group), device_id_type=MESH)
    for peer in group_peers:
        pl.semaphore_signal(barrier, inc=1, device_id=(region, peer), device_id_type=MESH)

    def region_copy(box, send, recv, owner, peer, send_slot):
        return pltpu.make_async_remote_copy(
            src_ref=box.at[owner], dst_ref=box.at[owner],
            send_sem=send.at[send_slot], recv_sem=recv.at[owner],
            device_id=(peer, group), device_id_type=MESH,
        )

    def group_copy(box, send, recv, owner, peer, send_slot):
        return pltpu.make_async_remote_copy(
            src_ref=box.at[owner], dst_ref=box.at[owner],
            send_sem=send.at[send_slot], recv_sem=recv.at[owner],
            device_id=(region, peer), device_id_type=MESH,
        )

    pending = []

    def exchange(copy, me, peers, box, send, recv):
        for slot, peer in enumerate(peers):
            sent = copy(box, send, recv, me, peer, slot)
            sent.start()
            pending.append(sent)

    def arrive(copy, peers, box, send, recv):
        for slot, peer in enumerate(peers):
            copy(box, send, recv, peer, peer, slot).wait_recv()

    for load in loads[4:]:
        load.wait()
    lane = lax.broadcasted_iota(jnp.int32, (SUB, LANES), 1)
    sub = lax.broadcasted_iota(jnp.int32, (SUB, LANES), 0)
    rows_of, cols_of = [], []
    col_marks = jnp.full((SUB, LANES), -1, jnp.int32)
    row_marks = jnp.full((SUB, LANES), -1, jnp.int32)
    for s in range(SUB):
        rows_of.append(tile_rows[0, 0, s])
        cols_of.append(tile_cols[0, 0, s])
        mine = jnp.logical_and(lane % SUB == s, s < jnp.full((SUB, LANES), tile_count[0, 0]))
        col_marks = jnp.where(mine, cols_of[s] * chunks + (lane // SUB) % chunks, col_marks)
        row_marks = jnp.where(mine, rows_of[s], row_marks)

    weight = jnp.full((1, 1), balance[0, 0], jnp.float32)
    half = SUB * chunks

    for iteration in range(ITERS):
        cbox, csend, crecv = col_box.at[iteration], col_send.at[iteration], col_recv.at[iteration]
        rbox, rsend, rrecv = row_box.at[iteration], row_send.at[iteration], row_recv.at[iteration]
        dual_step = step_scale * weight

        if iteration == 0:
            loads[0].wait()
        for s in range(SUB):
            dual_rows[s] = y[rows_of[s]]
        picked = dual_rows[...]
        diagonal = jnp.concatenate([jnp.where(sub == s, picked, 0.0) for s in range(SUB)], axis=1)
        if iteration == 0:
            loads[1].wait()
        products = unstacked(
            jnp.dot(stacked(diagonal), tiles[...], preferred_element_type=jnp.float32)
        )
        if iteration == 0:
            pl.semaphore_wait(barrier, regions + groups - 2)
        for k in range(chunks):
            cbox[region, k * SUB : (k + 1) * SUB, :] = products[:, k * LANES : (k + 1) * LANES]
        if iteration == 0:
            cbox[region, half : half + 1, :] = col_marks[:1].astype(jnp.float32)
        else:
            cbox[region, half : half + 1, :] = dual_moves
        exchange(region_copy, region, region_peers, cbox, csend, crecv)
        if iteration == 0:
            loads[2].wait()
            loads[3].wait()
        arrive(region_copy, region_peers, cbox, csend, crecv)

        if iteration == 0:
            place = lax.broadcasted_iota(jnp.int32, (x.shape[0], LANES), 0).astype(jnp.float32)
            spot = lax.broadcasted_iota(jnp.int32, (1, LANES), 1)
            per = LANES // half
            for j in range(regions // per):
                marks = cbox[j * per, half : half + 1, :]
                for i in range(1, per):
                    marks = jnp.where(spot // half == i, cbox[j * per + i, half : half + 1, :], marks)
                col_picks[:, j * LANES : (j + 1) * LANES] = jnp.where(
                    place == marks, 1.0, 0.0
                ).astype(jnp.bfloat16)
        else:
            dual_total = cbox[0, half : half + 1, :]
            for r in range(1, regions):
                dual_total = dual_total + cbox[r, half : half + 1, :]
            dual_total = jnp.sum(dual_total, axis=(0, 1), keepdims=True)
            weight = jnp.sqrt(
                weight * jnp.sqrt((dual_total + epsilon) / (primal_total + epsilon))
            )
            dual_step = step_scale * weight
        primal_step = step_scale / weight
        blocks = jnp.concatenate([cbox[r, :half, :] for r in range(regions)], axis=0)
        col_total = scatter(col_picks[...], blocks)
        before = x[...]
        moved = jnp.clip(before - primal_step * (cost[...] - col_total), 0.0, 1.0)
        x[...] = moved
        extrapolated[...] = (2.0 * moved - before).reshape(extrapolated.shape)
        if iteration == ITERS - 1:
            stores = [pltpu.make_async_copy(x, primal_out, store_sem.at[0])]
            stores[0].start()

        for s in range(SUB):
            primal_cols[s * chunks : (s + 1) * chunks, :] = extrapolated[cols_of[s]]
        routes = jnp.concatenate(
            [primal_cols[pl.ds(k, SUB, stride=chunks), :] for k in range(chunks)], axis=1
        )
        products = unstacked(
            lax.dot_general(
                stacked(routes), tiles[...], (((1,), (1,)), ((), ())),
                preferred_element_type=jnp.float32,
            )
        )
        own = jnp.where(sub == 0, products[:, :LANES], 0.0)
        for s in range(1, SUB):
            own = jnp.where(sub == s, products[:, s * LANES : (s + 1) * LANES], own)
        rbox[group, :SUB, :] = own
        rbox[group, SUB : SUB + 1, :] = folded((moved - before) ** 2)
        rbox[group, SUB + 1 : SUB + 2, :] = row_marks[:1].astype(jnp.float32)
        exchange(group_copy, group, group_peers, rbox, rsend, rrecv)
        arrive(group_copy, group_peers, rbox, rsend, rrecv)

        if iteration == 0:
            span = row_picks.shape[1]
            piece = min(span, LANES)
            place = lax.broadcasted_iota(jnp.int32, (y.shape[0], piece), 0).astype(jnp.float32)
            spot = lax.broadcasted_iota(jnp.int32, (1, piece), 1)
            per = piece // SUB
            for j in range(span // piece):
                marks = rbox[j * per, SUB + 1 : SUB + 2, :piece]
                for i in range(1, per):
                    marks = jnp.where(
                        spot // SUB == i, rbox[j * per + i, SUB + 1 : SUB + 2, :piece], marks
                    )
                row_picks[:, j * piece : (j + 1) * piece] = jnp.where(
                    place == marks, 1.0, 0.0
                ).astype(jnp.bfloat16)
        blocks = jnp.concatenate([rbox[c, :SUB, :] for c in range(groups)], axis=0)
        coverage = scatter(row_picks[...], blocks)
        held = y[...]
        updated = held + dual_step * (1.0 - coverage)
        y[...] = updated
        dual_moves = folded((updated - held) ** 2)
        if iteration == ITERS - 1:
            last_box[region, :, :] = dual_moves
            exchange(region_copy, region, region_peers, last_box, last_send, last_recv)
            stores.append(pltpu.make_async_copy(y, duals_out, store_sem.at[1]))
            stores[1].start()
        primal_total = rbox[0, SUB : SUB + 1, :]
        for c in range(1, groups):
            primal_total = primal_total + rbox[c, SUB : SUB + 1, :]
        primal_total = jnp.sum(primal_total, axis=(0, 1), keepdims=True)

    arrive(region_copy, region_peers, last_box, last_send, last_recv)
    dual_total = last_box[0]
    for r in range(1, regions):
        dual_total = dual_total + last_box[r]
    dual_total = jnp.sum(dual_total, axis=(0, 1), keepdims=True)
    final_weight[...] = jnp.sqrt(
        weight * jnp.sqrt((dual_total + epsilon) / (primal_total + epsilon))
    )
    stores.append(pltpu.make_async_copy(final_weight, balance_out, store_sem.at[2]))
    stores[2].start()
    for sent in pending:
        sent.wait_send()
    for store in stores:
        store.wait()


def handed_over(*refs):
    for i in range(3):
        refs[3 + i][...] = refs[i][...]


def local(regions, groups, incidence, tile_rows, tile_cols, tile_count, route_cost, primal, duals, balance):
    slots, height, width = incidence.shape[2:]
    assert slots == SUB and height == LANES and width % LANES == 0
    chunks = width // LANES
    wide = (primal.shape[0] // LANES, LANES)
    tall = (duals.shape[0] // LANES, LANES)
    f32 = jnp.float32
    dma = pltpu.SemaphoreType.DMA
    hbm = pl.BlockSpec(memory_space=pltpu.HBM)
    outs = pl.pallas_call(
        functools.partial(kernel, regions, groups),
        out_shape=(
            jax.ShapeDtypeStruct(wide, f32),
            jax.ShapeDtypeStruct(tall, f32),
            jax.ShapeDtypeStruct((1, 1), f32),
        ),
        in_specs=[hbm] * 8,
        out_specs=(hbm, hbm, hbm),
        scratch_shapes=[
            pltpu.SMEM(tile_rows.shape, jnp.int32),
            pltpu.SMEM(tile_cols.shape, jnp.int32),
            pltpu.SMEM(tile_count.shape, jnp.int32),
            pltpu.SMEM((1, 1), f32),
            pltpu.VMEM((slots * height, width), jnp.bfloat16),
            pltpu.VMEM(wide, f32),
            pltpu.VMEM(wide, f32),
            pltpu.VMEM(tall, f32),
            pltpu.VMEM((wide[0] // chunks, chunks, LANES), f32),
            pltpu.VMEM((SUB, LANES), f32),
            pltpu.VMEM((slots * chunks, LANES), f32),
            pltpu.VMEM((wide[0], regions * slots * chunks), jnp.bfloat16),
            pltpu.VMEM((tall[0], groups * slots), jnp.bfloat16),
            pltpu.VMEM((ITERS, regions, slots * chunks + 1, LANES), f32),
            pltpu.VMEM((ITERS, groups, SUB + 2, LANES), f32),
            pltpu.VMEM((regions, 1, LANES), f32),
            pltpu.VMEM((1, 1), f32),
            dma((8,)),
            dma((3,)),
            dma((ITERS, regions)),
            dma((ITERS, regions)),
            dma((ITERS, groups)),
            dma((ITERS, groups)),
            dma((regions,)),
            dma((regions,)),
        ],
        compiler_params=pltpu.CompilerParams(
            collective_id=0, has_side_effects=True, vmem_limit_bytes=56 * 1024 * 1024
        ),
    )(
        tile_rows, tile_cols, tile_count, balance.reshape(1, 1),
        incidence.reshape(slots * height, width),
        route_cost.reshape(wide), primal.reshape(wide), duals.reshape(tall),
    )
    outs = pl.pallas_call(
        handed_over,
        out_shape=tuple(jax.ShapeDtypeStruct(out.shape, f32) for out in outs),
    )(*outs)
    return outs[0].reshape(-1), outs[1].reshape(-1), outs[2].reshape(())


def solution(mesh):
    return jax.shard_map(
        functools.partial(local, mesh.shape["region"], mesh.shape["cols"]),
        mesh=mesh,
        in_specs=(
            P("region", "cols", None, None, None),
            P("region", "cols", None),
            P("region", "cols", None),
            P("region", "cols"),
            P("cols"),
            P("cols"),
            P("region"),
            P(),
        ),
        out_specs=(P("cols"), P("region"), P()),
        check_vma=False,
    )
```

```python
import functools

import jax
import jax.numpy as jnp
from jax import lax
from jax.experimental import pallas as pl
from jax.experimental.pallas import tpu as pltpu
from jax.sharding import PartitionSpec as P

ITERS = 2

step_scale = 0.012
epsilon = 1e-06
MESH = pl.DeviceIdType.MESH
LANES = 128
SUB = 8


def split(value):
    high = value.astype(jnp.bfloat16).astype(jnp.float32)
    rest = value - high
    middle = rest.astype(jnp.bfloat16).astype(jnp.float32)
    return high, middle, rest - middle


def stacked(value):
    high, middle, low = split(value)
    rows = jnp.concatenate([high, middle, low, jnp.zeros_like(value)], axis=0)
    return rows.astype(jnp.bfloat16)


def unstacked(product):
    return product[2 * SUB : 3 * SUB] + product[SUB : 2 * SUB] + product[:SUB]


def scatter(picks, blocks):
    sides = [term.astype(jnp.bfloat16) for term in split(blocks)]
    product = jnp.dot(
        picks, jnp.concatenate(sides, axis=1), preferred_element_type=jnp.float32
    )
    return product[:, 2 * LANES :] + product[:, LANES : 2 * LANES] + product[:, :LANES]


def folded(value):
    return jnp.sum(jnp.sum(value.reshape(-1, SUB, LANES), axis=0), axis=0, keepdims=True)


def kernel(
    regions, groups,
    tile_rows_hbm, tile_cols_hbm, tile_count_hbm, balance_hbm,
    incidence_hbm, cost_hbm, primal_hbm, duals_hbm,
    primal_out, duals_out, balance_out,
    tile_rows, tile_cols, tile_count, balance,
    tiles, cost, x, y, extrapolated, dual_rows, primal_cols,
    col_picks, row_picks, col_box, row_box, last_box, final_weight,
    load_sem, store_sem,
    col_send, col_recv, row_send, row_recv, last_send, last_recv,
):
    region, group = lax.axis_index("region"), lax.axis_index("cols")
    width = tiles.shape[1]
    chunks = width // LANES

    region_peers = [lax.rem(region + d, regions) for d in range(1, regions)]
    group_peers = [lax.rem(group + d, groups) for d in range(1, groups)]
    barrier = pltpu.get_barrier_semaphore()
    for peer in region_peers:
        pl.semaphore_signal(barrier, inc=1, device_id=(peer, group), device_id_type=MESH)
    for peer in group_peers:
        pl.semaphore_signal(barrier, inc=1, device_id=(region, peer), device_id_type=MESH)

    loads = [
        pltpu.make_async_copy(source, target, load_sem.at[i])
        for i, (source, target) in enumerate(
            (
                (duals_hbm, y), (incidence_hbm, tiles), (primal_hbm, x), (cost_hbm, cost),
                (tile_rows_hbm, tile_rows), (tile_cols_hbm, tile_cols),
                (tile_count_hbm, tile_count), (balance_hbm, balance),
            )
        )
    ]
    for load in loads[4:] + loads[:4]:
        load.start()

    def region_copy(box, send, recv, owner, peer, send_slot):
        return pltpu.make_async_remote_copy(
            src_ref=box.at[owner], dst_ref=box.at[owner],
            send_sem=send.at[send_slot], recv_sem=recv.at[owner],
            device_id=(peer, group), device_id_type=MESH,
        )

    def group_copy(box, send, recv, owner, peer, send_slot):
        return pltpu.make_async_remote_copy(
            src_ref=box.at[owner], dst_ref=box.at[owner],
            send_sem=send.at[send_slot], recv_sem=recv.at[owner],
            device_id=(region, peer), device_id_type=MESH,
        )

    pending = []

    def exchange(copy, me, peers, box, send, recv):
        for slot, peer in enumerate(peers):
            sent = copy(box, send, recv, me, peer, slot)
            sent.start()
            pending.append(sent)

    def arrive(copy, peers, box, send, recv):
        for slot, peer in enumerate(peers):
            copy(box, send, recv, peer, peer, slot).wait_recv()

    for load in loads[4:]:
        load.wait()
    lane = lax.broadcasted_iota(jnp.int32, (SUB, LANES), 1)
    sub = lax.broadcasted_iota(jnp.int32, (SUB, LANES), 0)
    rows_of, cols_of = [], []
    col_marks = jnp.full((SUB, LANES), -1, jnp.int32)
    row_marks = jnp.full((SUB, LANES), -1, jnp.int32)
    for s in range(SUB):
        rows_of.append(tile_rows[0, 0, s])
        cols_of.append(tile_cols[0, 0, s])
        mine = jnp.logical_and(lane % SUB == s, s < jnp.full((SUB, LANES), tile_count[0, 0]))
        col_marks = jnp.where(mine, cols_of[s] * chunks + (lane // SUB) % chunks, col_marks)
        row_marks = jnp.where(mine, rows_of[s], row_marks)

    weight = jnp.full((1, 1), balance[0, 0], jnp.float32)
    half = SUB * chunks

    for iteration in range(ITERS):
        cbox, csend, crecv = col_box.at[iteration], col_send.at[iteration], col_recv.at[iteration]
        rbox, rsend, rrecv = row_box.at[iteration], row_send.at[iteration], row_recv.at[iteration]
        dual_step = step_scale * weight

        if iteration == 0:
            loads[0].wait()
        for s in range(SUB):
            dual_rows[s] = y[rows_of[s]]
        picked = dual_rows[...]
        diagonal = jnp.concatenate([jnp.where(sub == s, picked, 0.0) for s in range(SUB)], axis=1)
        if iteration == 0:
            loads[1].wait()
        products = unstacked(
            jnp.dot(stacked(diagonal), tiles[...], preferred_element_type=jnp.float32)
        )
        if iteration == 0:
            pl.semaphore_wait(barrier, regions + groups - 2)
        for k in range(chunks):
            cbox[region, k * SUB : (k + 1) * SUB, :] = products[:, k * LANES : (k + 1) * LANES]
        if iteration == 0:
            cbox[region, half : half + 1, :] = col_marks[:1].astype(jnp.float32)
        else:
            cbox[region, half : half + 1, :] = dual_moves
        exchange(region_copy, region, region_peers, cbox, csend, crecv)
        if iteration == 0:
            loads[2].wait()
            loads[3].wait()
        arrive(region_copy, region_peers, cbox, csend, crecv)

        if iteration == 0:
            place = lax.broadcasted_iota(jnp.int32, (x.shape[0], LANES), 0).astype(jnp.float32)
            spot = lax.broadcasted_iota(jnp.int32, (1, LANES), 1)
            per = LANES // half
            for j in range(regions // per):
                marks = cbox[j * per, half : half + 1, :]
                for i in range(1, per):
                    marks = jnp.where(spot // half == i, cbox[j * per + i, half : half + 1, :], marks)
                col_picks[:, j * LANES : (j + 1) * LANES] = jnp.where(
                    place == marks, 1.0, 0.0
                ).astype(jnp.bfloat16)
        else:
            dual_total = cbox[0, half : half + 1, :]
            for r in range(1, regions):
                dual_total = dual_total + cbox[r, half : half + 1, :]
            dual_total = jnp.sum(dual_total, axis=(0, 1), keepdims=True)
            weight = jnp.sqrt(
                weight * jnp.sqrt((dual_total + epsilon) / (primal_total + epsilon))
            )
            dual_step = step_scale * weight
        primal_step = step_scale / weight
        blocks = jnp.concatenate([cbox[r, :half, :] for r in range(regions)], axis=0)
        col_total = scatter(col_picks[...], blocks)
        before = x[...]
        moved = jnp.clip(before - primal_step * (cost[...] - col_total), 0.0, 1.0)
        x[...] = moved
        extrapolated[...] = (2.0 * moved - before).reshape(extrapolated.shape)
        if iteration == ITERS - 1:
            stores = [pltpu.make_async_copy(x, primal_out, store_sem.at[0])]
            stores[0].start()

        for s in range(SUB):
            primal_cols[s * chunks : (s + 1) * chunks, :] = extrapolated[cols_of[s]]
        routes = jnp.concatenate(
            [primal_cols[pl.ds(k, SUB, stride=chunks), :] for k in range(chunks)], axis=1
        )
        products = unstacked(
            lax.dot_general(
                stacked(routes), tiles[...], (((1,), (1,)), ((), ())),
                preferred_element_type=jnp.float32,
            )
        )
        own = jnp.where(sub == 0, products[:, :LANES], 0.0)
        for s in range(1, SUB):
            own = jnp.where(sub == s, products[:, s * LANES : (s + 1) * LANES], own)
        rbox[group, :SUB, :] = own
        rbox[group, SUB : SUB + 1, :] = folded((moved - before) ** 2)
        rbox[group, SUB + 1 : SUB + 2, :] = row_marks[:1].astype(jnp.float32)
        exchange(group_copy, group, group_peers, rbox, rsend, rrecv)
        arrive(group_copy, group_peers, rbox, rsend, rrecv)

        if iteration == 0:
            span = row_picks.shape[1]
            piece = min(span, LANES)
            place = lax.broadcasted_iota(jnp.int32, (y.shape[0], piece), 0).astype(jnp.float32)
            spot = lax.broadcasted_iota(jnp.int32, (1, piece), 1)
            per = piece // SUB
            for j in range(span // piece):
                marks = rbox[j * per, SUB + 1 : SUB + 2, :piece]
                for i in range(1, per):
                    marks = jnp.where(
                        spot // SUB == i, rbox[j * per + i, SUB + 1 : SUB + 2, :piece], marks
                    )
                row_picks[:, j * piece : (j + 1) * piece] = jnp.where(
                    place == marks, 1.0, 0.0
                ).astype(jnp.bfloat16)
        blocks = jnp.concatenate([rbox[c, :SUB, :] for c in range(groups)], axis=0)
        coverage = scatter(row_picks[...], blocks)
        held = y[...]
        updated = held + dual_step * (1.0 - coverage)
        y[...] = updated
        dual_moves = folded((updated - held) ** 2)
        if iteration == ITERS - 1:
            last_box[region, :, :] = dual_moves
            exchange(region_copy, region, region_peers, last_box, last_send, last_recv)
            stores.append(pltpu.make_async_copy(y, duals_out, store_sem.at[1]))
            stores[1].start()
        primal_total = rbox[0, SUB : SUB + 1, :]
        for c in range(1, groups):
            primal_total = primal_total + rbox[c, SUB : SUB + 1, :]
        primal_total = jnp.sum(primal_total, axis=(0, 1), keepdims=True)

    arrive(region_copy, region_peers, last_box, last_send, last_recv)
    dual_total = last_box[0]
    for r in range(1, regions):
        dual_total = dual_total + last_box[r]
    dual_total = jnp.sum(dual_total, axis=(0, 1), keepdims=True)
    final_weight[...] = jnp.sqrt(
        weight * jnp.sqrt((dual_total + epsilon) / (primal_total + epsilon))
    )
    stores.append(pltpu.make_async_copy(final_weight, balance_out, store_sem.at[2]))
    stores[2].start()
    for sent in pending:
        sent.wait_send()
    for store in stores:
        store.wait()


def local(regions, groups, incidence, tile_rows, tile_cols, tile_count, route_cost, primal, duals, balance):
    slots, height, width = incidence.shape[2:]
    assert slots == SUB and height == LANES and width % LANES == 0
    chunks = width // LANES
    wide = (primal.shape[0] // LANES, LANES)
    tall = (duals.shape[0] // LANES, LANES)
    f32 = jnp.float32
    dma = pltpu.SemaphoreType.DMA
    hbm = pl.BlockSpec(memory_space=pltpu.HBM)
    outs = pl.pallas_call(
        functools.partial(kernel, regions, groups),
        out_shape=(
            pltpu.VMEM(wide, f32),
            pltpu.VMEM(tall, f32),
            pltpu.VMEM((1, 1), f32),
        ),
        in_specs=[hbm] * 8,
        out_specs=(pl.BlockSpec(memory_space=pl.ANY),) * 3,
        scratch_shapes=[
            pltpu.SMEM(tile_rows.shape, jnp.int32),
            pltpu.SMEM(tile_cols.shape, jnp.int32),
            pltpu.SMEM(tile_count.shape, jnp.int32),
            pltpu.SMEM((1, 1), f32),
            pltpu.VMEM((slots * height, width), jnp.bfloat16),
            pltpu.VMEM(wide, f32),
            pltpu.VMEM(wide, f32),
            pltpu.VMEM(tall, f32),
            pltpu.VMEM((wide[0] // chunks, chunks, LANES), f32),
            pltpu.VMEM((SUB, LANES), f32),
            pltpu.VMEM((slots * chunks, LANES), f32),
            pltpu.VMEM((wide[0], regions * slots * chunks), jnp.bfloat16),
            pltpu.VMEM((tall[0], groups * slots), jnp.bfloat16),
            pltpu.VMEM((ITERS, regions, slots * chunks + 1, LANES), f32),
            pltpu.VMEM((ITERS, groups, SUB + 2, LANES), f32),
            pltpu.VMEM((regions, 1, LANES), f32),
            pltpu.VMEM((1, 1), f32),
            dma((8,)),
            dma((3,)),
            dma((ITERS, regions)),
            dma((ITERS, regions)),
            dma((ITERS, groups)),
            dma((ITERS, groups)),
            dma((regions,)),
            dma((regions,)),
        ],
        compiler_params=pltpu.CompilerParams(
            collective_id=0, has_side_effects=True, vmem_limit_bytes=56 * 1024 * 1024
        ),
    )(
        tile_rows, tile_cols, tile_count, balance.reshape(1, 1),
        incidence.reshape(slots * height, width),
        route_cost.reshape(wide), primal.reshape(wide), duals.reshape(tall),
    )
    return outs[0].reshape(-1), outs[1].reshape(-1), outs[2].reshape(())


def solution(mesh):
    return jax.shard_map(
        functools.partial(local, mesh.shape["region"], mesh.shape["cols"]),
        mesh=mesh,
        in_specs=(
            P("region", "cols", None, None, None),
            P("region", "cols", None),
            P("region", "cols", None),
            P("region", "cols"),
            P("cols"),
            P("cols"),
            P("region"),
            P(),
        ),
        out_specs=(P("cols"), P("region"), P()),
        check_vma=False,
    )
```
